32 devices in a mesh: pipe: 2 (over y), expert: 4 (over z), tensor: 4 (over x, core).
Axes of the slice: x: 2, y: 2, z: 4, core: 2. Of those that a mesh axis runs over, the one named last changes fastest.
Arguments:
- x_branch: bfloat16 [640, 16384], P('expert', ('pipe', 'tensor')), may hold values from -6 to 6
- z_branch: bfloat16 [640, 16384], P('expert', ('pipe', 'tensor')), may hold values from -6 to 6
- step_raw: bfloat16 [640, 16384], P('expert', ('pipe', 'tensor')), may hold values from -6 to 6
- b_matrix: float32 [640, 16], P('expert'), may hold values from -6 to 6
- c_matrix: float32 [640, 16], P('expert'), may hold values from -1.5 to 1.5
- conv_weight: float32 [4, 16384], P(None, ('pipe', 'tensor')), may hold values from -3 to 3
- conv_bias: float32 [16384], P(('pipe', 'tensor')), may hold values from -3 to 3
- step_bias: float32 [16384], P(('pipe', 'tensor')), may hold values from -4 to -0.5
- a_log: float32 [16384, 16], P(('pipe', 'tensor')), may hold values from -4 to 1.5
- skip: float32 [16384], P(('pipe', 'tensor')), may hold values from 0.5 to 1.5
- w_out: bfloat16 [4096, 16384], P(('pipe', 'tensor')), may hold values from -0.046875 to 0.046875
- residual: bfloat16 [640, 4096], P('expert', ('pipe', 'tensor')), may hold values from -41 to 41
- norm_gain: float32 [4096], replicated, may hold values from 0.5 to 1.5
- expert_ids: int32 [640, 2], P('expert'), may hold values from 0 to 3, all different within a row; in each aligned block of 160 rows (0 to 159, 160 to 319, ...) at most 120 rows name the same one
- gate_probs: float32 [640, 2], P('expert'), may hold values from 0.2 to 1
- w_gate: bfloat16 [4, 16384, 4096], P('expert', 'tensor', 'pipe'), may hold values from -0.09375 to 0.09375
- w_up: bfloat16 [4, 16384, 4096], P('expert', 'tensor', 'pipe'), may hold values from -0.09375 to 0.09375
- w_down: bfloat16 [4, 16384, 4096], P('expert', 'tensor', 'pipe'), may hold values from -0.046875 to 0.046875
Outputs:
- mixed: bfloat16 [640, 4096], P('expert', ('pipe', 'tensor'))
The draws below stay inside these ranges and needn't reach their ends.
Inputs may be any that keep to these rules, and one draw needn't show every extreme that they name: `expert_ids`: the two experts of a token differ. The 160 rows of one sequence name any one expert at most 120 times, and in every draw some sequence names some expert exactly 120 times.
All inputs are finite; a program needn't handle non-finite values.
Results may differ from the reference program's by a relative error of at most 0.0053.
Values may be sent and summed in bfloat16 or wider, within the bound.
A program may use at most 320 MiB of HBM per device.

```python
import math
import jax
import jax.numpy as jnp
import numpy as np
from jax import lax

D = 4096
E = 16384
STATE = 16
KCONV = 4
FF = 16384
TOP = 2
TOK = 160
CAP = 120
EXPERTS = 4
TOKENS = 640
N_EXPERT = 4


def draw_residual(key, part):
    first_key = jax.random.fold_in(jax.random.fold_in(key, 17), 0)
    columns = jnp.arange(D, dtype=jnp.float32) / D
    column_scale = jnp.exp(jnp.log(3.0) * columns)
    values = jnp.clip(jax.random.normal(first_key, (TOKENS, D), jnp.float32), -6.0, 6.0)
    return (values * column_scale).astype(jnp.bfloat16)


def steps_of(rng, dims, shards, smallest, high):
    gain, own = 1.0, jax.random.fold_in(rng, 6)
    for position, blocks in shards:
        heights = jnp.exp(jax.random.uniform(jax.random.fold_in(own, position), (blocks,), jnp.float32, smallest / len(shards), high / len(shards)))
        gain = gain * jnp.repeat(heights, dims[position] // blocks).reshape([-1 if axis == position else 1 for axis in range(len(dims))])
    return gain


def shared_out(stream_key, own, number, rows, number_of, top, limit, lean):
    ranking = jax.random.permutation(stream_key, number_of)
    packed, common = shares(number_of, rows * top, limit, lean, True), shares(number_of, rows * top, limit, lean, False)
    places = jnp.arange(number_of)

    def named(lengths, rotation):
        used = int((lengths > 0).sum())
        fixed = max(1, used // 4)
        shifted = fixed + (places - fixed + rotation * (used - fixed)) % max(1, number_of - fixed)
        return jnp.zeros((number_of,), jnp.int32).at[ranking[jnp.where(places < fixed, places, shifted)]].set(jnp.asarray(lengths, jnp.int32))

    lengths = jnp.where(number % 4 == 0, named(packed, number // 4), named(common, number - number // 4 - 1))
    mixed = jax.random.permutation(jax.random.fold_in(own, 3), number_of)
    source_of, sink = mixed[0:number_of // 2 * 2:2], mixed[1:number_of // 2 * 2:2]
    margin = jnp.minimum(lengths[source_of] - 1, limit - lengths[sink]) // 2
    margin = jnp.where((source_of == ranking[0]) | (sink == ranking[0]) | (lengths[sink] == 0), 0, jnp.maximum(margin, 0))
    shifted = jax.random.randint(jax.random.fold_in(own, 4), (number_of // 2,), 0, 1 << 20) % (margin + 1)
    lengths = lengths.at[source_of].add(-shifted).at[sink].add(shifted)
    labels = jnp.searchsorted(jnp.cumsum(lengths), jnp.arange(rows * top), side="right").astype(jnp.int32)
    grid = labels.reshape(top, rows).T
    grid = grid[jax.random.permutation(jax.random.fold_in(own, 1), rows)]
    rotation = jax.random.randint(jax.random.fold_in(own, 2), (rows, 1), 0, top)
    return jnp.take_along_axis(grid, (jnp.arange(top)[None, :] + rotation) % top, axis=1)


def shares(count, total, limit, lean, full):
    loads = [(1 << 20) // math.isqrt(grade ** lean) + 1 for grade in range(1, count + 1)]
    largest = limit if full else min(limit, max(-(-total // count), total * loads[0] // sum(loads)))
    least = 1 if total - largest >= count - 1 else 0
    given, rest = [largest] + [least] * (count - 1), total - largest - least * (count - 1)
    while rest > 0:
        movable = [i for i in range(1, count) if given[i] < largest] or [i for i in range(1, count) if given[i] < limit]
        whole, budget = sum([loads[i] for i in movable]), rest
        for i in movable:
            more = min(limit - given[i], max(1, budget * loads[i] // whole), rest)
            given[i] = given[i] + more
            rest = rest - more
    return np.array(given)


def noise(rng, shape, scale, bound, cuts=(), kind=jnp.bfloat16):
    drawn = jax.random.normal(rng, shape, jnp.float32) * scale
    if len(cuts) > 0:
        drawn = steps_of(rng, shape, cuts, -0.22, 0.18) * drawn
    return jnp.clip(drawn, min=-bound, max=bound).astype(kind)


def setup_inputs(seed: int = 0) -> dict:
    streams_of = jax.random.split(jax.random.key(seed), 19)
    x_branch = noise(streams_of[0], (TOKENS, E), 1.0, 6.0, ((0, 4), (1, 8)))
    z_branch = noise(streams_of[1], (TOKENS, E), 1.0, 6.0, ((0, 4), (1, 8)))
    step_raw = noise(streams_of[2], (TOKENS, E), 1.5, 6.0, ((0, 4), (1, 8)))
    b_matrix = noise(streams_of[3], (TOKENS, STATE), 1.0, 6.0, ((0, 4),), jnp.float32)
    c_matrix = noise(streams_of[4], (TOKENS, STATE), 0.25, 1.5, ((0, 4),), jnp.float32)
    conv_weight = noise(streams_of[5], (KCONV, E), KCONV ** -0.5, 3.0, ((1, 8),), jnp.float32)
    conv_bias = noise(streams_of[6], (E,), 0.5, 3.0, ((0, 8),), jnp.float32)
    step_bias = jnp.clip(-4.0 + 3.5 * jax.random.uniform(streams_of[7], (E,), jnp.float32) ** steps_of(streams_of[7], (E,), ((0, 8),), -0.2, 0.2), -4.0, -0.5)
    a_log = jnp.clip(-4.0 + 5.5 * jax.random.uniform(streams_of[8], (E, STATE), jnp.float32) ** steps_of(streams_of[8], (E, STATE), ((0, 8),), -0.2, 0.2), -4.0, 1.5)
    skip = jnp.clip(1.0 + 0.1 * jax.random.normal(streams_of[9], (E,), jnp.float32), 0.5, 1.5)
    w_out = noise(streams_of[10], (D, E), E ** -0.5, 0.046875, ((0, 8),))
    residual = draw_residual(jax.random.fold_in(streams_of[18], 71), 0)
    norm_gain = jnp.clip(1.0 + 0.1 * jax.random.normal(streams_of[12], (D,), jnp.float32), 0.5, 1.5)
    expert_ids_keys = jax.random.split(jax.random.fold_in(streams_of[13], 1), TOKENS // TOK)
    expert_ids_turns = jax.random.permutation(jax.random.fold_in(streams_of[13], 3), TOKENS // TOK)
    expert_ids = jax.vmap(lambda own, number: shared_out(jax.random.fold_in(streams_of[13], 2), own, number, TOK, EXPERTS, TOP, CAP, 2))(expert_ids_keys, expert_ids_turns).reshape((TOKENS, TOP))
    gate_probs = jnp.clip(0.2 + 0.8 * jax.random.uniform(streams_of[14], (TOKENS, TOP), jnp.float32) ** steps_of(streams_of[14], (TOKENS, TOP), ((0, 4),), -0.2, 0.2), 0.2, 1.0)
    w_gate = noise(streams_of[15], (EXPERTS, FF, D), D ** -0.5, 0.09375, ((0, 4), (1, 4), (2, 2)))
    w_up = noise(streams_of[16], (EXPERTS, FF, D), D ** -0.5, 0.09375, ((0, 4), (1, 4), (2, 2)))
    w_down = noise(streams_of[17], (EXPERTS, FF, D), FF ** -0.5, 0.046875, ((0, 4), (1, 4), (2, 2)))
    return dict(x_branch=x_branch, z_branch=z_branch, step_raw=step_raw, b_matrix=b_matrix, c_matrix=c_matrix, conv_weight=conv_weight, conv_bias=conv_bias, step_bias=step_bias, a_log=a_log, skip=skip, w_out=w_out, residual=residual, norm_gain=norm_gain, expert_ids=expert_ids, gate_probs=gate_probs, w_gate=w_gate, w_up=w_up, w_down=w_down)


EPSILON = 1e-05

def scan_states(steps_dt, inner, b_seq, c_seq, rates):

    def advance(state, inputs):
        dt_now, inner_now, b_now, c_now = inputs
        state = jnp.exp(dt_now[:, :, None] * rates[None, :, :]) * state + (dt_now * inner_now)[:, :, None] * b_now[:, None, :]
        return (state, lax.optimization_barrier(jnp.sum(state * c_now[:, None, :], axis=2)))
    start_state = jnp.zeros((steps_dt.shape[0], steps_dt.shape[2], rates.shape[1]), jnp.float32)
    moved = (jnp.swapaxes(steps_dt, 0, 1), jnp.swapaxes(inner, 0, 1), jnp.swapaxes(b_seq, 0, 1), jnp.swapaxes(c_seq, 0, 1))
    _, readout = lax.scan(advance, start_state, moved)
    return jnp.swapaxes(readout, 0, 1)

def reference(x_branch, z_branch, step_raw, b_matrix, c_matrix, conv_weight, conv_bias, step_bias, a_log, skip, w_out, residual, norm_gain, expert_ids, gate_probs, w_gate, w_up, w_down):
    values = x_branch.astype(jnp.float32).reshape(N_EXPERT, TOK, E)
    padded = jnp.pad(values, ((0, 0), (KCONV - 1, 0), (0, 0)))
    conv = conv_bias + conv_weight[0] * padded[:, 0:TOK, :]
    for offset in range(1, KCONV):
        conv = conv + conv_weight[offset] * padded[:, offset:offset + TOK, :]
    inner = jax.nn.silu(conv)
    steps_dt = jax.nn.softplus(step_raw.astype(jnp.float32).reshape(N_EXPERT, TOK, E) + step_bias)
    rates = -jnp.exp(a_log)
    readout = scan_states(steps_dt, inner, b_matrix.reshape(N_EXPERT, TOK, STATE), c_matrix.reshape(N_EXPERT, TOK, STATE), rates)
    gate_z = jax.nn.silu(z_branch.astype(jnp.float32).reshape(N_EXPERT, TOK, E))
    gated = ((readout + skip * inner) * gate_z).astype(jnp.bfloat16).reshape(TOKENS, E)
    mamba_out = jnp.dot(gated, w_out.T, preferred_element_type=jnp.float32)
    stream = (residual.astype(jnp.float32) + mamba_out).astype(jnp.bfloat16)
    stream_f = stream.astype(jnp.float32)
    inverse = lax.rsqrt(lax.optimization_barrier(jnp.sum(stream_f * stream_f, axis=1, keepdims=True)) / D + EPSILON)
    scaled = (stream_f * norm_gain).astype(jnp.bfloat16)

    def add_expert(total, index):
        gate_pre = inverse * jnp.dot(scaled, w_gate[index].T, preferred_element_type=jnp.float32)
        up_pre = inverse * jnp.dot(scaled, w_up[index].T, preferred_element_type=jnp.float32)
        hidden = (jax.nn.silu(gate_pre) * up_pre).astype(jnp.bfloat16)
        expert_out = jnp.dot(hidden, w_down[index], preferred_element_type=jnp.float32)
        weight = lax.optimization_barrier(jnp.sum(jnp.where(expert_ids == index, gate_probs, jnp.zeros_like(gate_probs)), axis=1))
        return (total + weight[:, None] * expert_out, None)
    start_total = jnp.zeros((TOKENS, D), jnp.float32)
    expert_mix, _ = lax.scan(add_expert, start_total, jnp.arange(EXPERTS, dtype=jnp.int32))
    return (stream_f + expert_mix).astype(jnp.bfloat16)
```

```python
import jax
import jax.numpy as jnp
import numpy as np
from jax import lax
from jax.experimental import pallas as pl
from jax.experimental.pallas import tpu as pltpu
from jax.sharding import PartitionSpec as P

D = 4096
CAP = 120
LANES = 128
EPSILON = 1e-05
LOG2_E = float(np.log2(np.e))


def scan_kernel(
    b_ref, c_ref, x_ref, z_ref, step_ref, taps_ref, bias_ref, step_bias_ref, a_log_ref, skip_ref,
    out_ref, padded, inner_ref, dt_ref, drive_ref, read_ref, rate_ref,
):
    length = x_ref.shape[0]
    states, rows, _ = a_log_ref.shape
    taps = taps_ref.shape[0]
    rate_ref[...] = -jnp.exp(a_log_ref[...]) * LOG2_E
    padded[0:8, :] = jnp.zeros((8, LANES), jnp.float32)
    for k in range(rows):
        cols = slice(k * LANES, (k + 1) * LANES)
        padded[8 : 8 + length, :] = x_ref[:, cols].astype(jnp.float32)
        conv = bias_ref[0:1, cols] + taps_ref[0:1, cols] * padded[9 - taps : 9 - taps + length, :]
        for offset in range(1, taps):
            begin = 9 - taps + offset
            conv = conv + taps_ref[offset : offset + 1, cols] * padded[begin : begin + length, :]
        inner = jax.nn.silu(conv)
        raw = step_ref[:, cols].astype(jnp.float32) + step_bias_ref[0:1, cols]
        dt = jnp.maximum(raw, 0.0) + jnp.log1p(jnp.exp(-jnp.abs(raw)))
        inner_ref[:, cols] = inner
        dt_ref[pl.ds(k, length, stride=rows), :] = dt
        drive_ref[pl.ds(k, length, stride=rows), :] = dt * inner

    def advance(t, state):
        here = pl.ds(pl.multiple_of(t * rows, rows), rows)
        dt, drive = dt_ref[here, :], drive_ref[here, :]
        later, sums = [], [None, None]
        for n in range(states):
            new = jnp.exp2(dt * rate_ref[n]) * state[n] + drive * b_ref[t, n]
            later.append(new)
            term = new * c_ref[t, n]
            sums[n % 2] = term if sums[n % 2] is None else sums[n % 2] + term
        read_ref[here, :] = sums[0] + sums[1]
        return tuple(later)

    lax.fori_loop(
        0, length, advance, tuple(jnp.zeros((rows, LANES), jnp.float32) for _ in range(states)), unroll=4
    )
    for k in range(rows):
        cols = slice(k * LANES, (k + 1) * LANES)
        read = read_ref[pl.ds(k, length, stride=rows), :] + skip_ref[0:1, cols] * inner_ref[:, cols]
        out_ref[:, cols] = (read * jax.nn.silu(z_ref[:, cols].astype(jnp.float32))).astype(out_ref.dtype)


def scan_block(index, rows, x, z, step, b, c, taps, bias, step_bias, a_log, skip):
    length, states = x.shape[0], a_log.shape[0]
    width = rows * LANES
    tall = pl.BlockSpec((length, width), lambda i: (0, index))
    flat = pl.BlockSpec((1, width), lambda i: (0, index))
    scalars = pl.BlockSpec(memory_space=pltpu.SMEM)
    wide = pltpu.VMEM((length * rows, LANES), jnp.float32)
    return pl.pallas_call(
        scan_kernel,
        grid=(1,),
        out_shape=jax.ShapeDtypeStruct((length, width), jnp.bfloat16),
        in_specs=[
            scalars, scalars, tall, tall, tall,
            pl.BlockSpec((taps.shape[0], width), lambda i: (0, index)), flat, flat,
            pl.BlockSpec((states, rows, LANES), lambda i: (0, index, 0)), flat,
        ],
        out_specs=pl.BlockSpec((length, width), lambda i: (0, 0)),
        scratch_shapes=[
            pltpu.VMEM((length + 8, LANES), jnp.float32),
            pltpu.VMEM((length, width), jnp.float32),
            wide, wide, wide,
            pltpu.VMEM((states, rows, LANES), jnp.float32),
        ],
        compiler_params=pltpu.CompilerParams(vmem_limit_bytes=32 * 2**20),
        cost_estimate=pl.CostEstimate(flops=10**10, bytes_accessed=2 * 10**6, transcendentals=0),
    )(b, c, x, z, step, taps, bias, step_bias, a_log, skip)


def contract_last(left, right):
    return lax.dot_general(left, right, (((1,), (1,)), ((), ())), preferred_element_type=jnp.float32)


def contract_first(left, right):
    return lax.dot_general(left, right, (((0,), (0,)), ((), ())), preferred_element_type=jnp.float32)


def swap(value, axis, mask):
    size = lax.axis_size(axis)
    return lax.ppermute(value, axis, [(i, i ^ mask) for i in range(size)])


def project(blocks, w_out):
    pipes, tensors = lax.axis_size("pipe"), lax.axis_size("tensor")
    count, width = len(blocks), blocks[0].shape[1]
    if (pipes, tensors) != (2, 4):
        whole = lax.all_gather(jnp.concatenate(blocks, axis=1), ("pipe", "tensor"), axis=1, tiled=True)
        return contract_last(whole, w_out)
    me = lax.axis_index("pipe") * tensors + lax.axis_index("tensor")
    total = None
    held = [[(block, 0)] for block in blocks]
    orders = [[("pipe", 1), ("tensor", 2), ("tensor", 1)], [("tensor", 2), ("pipe", 1), ("tensor", 1)]]
    for step in range(3):
        for index in range(count):
            axis, mask = orders[index % 2][step]
            own_mask = mask * tensors if axis == "pipe" else mask
            held[index] += [(swap(block, axis, mask), have ^ own_mask) for block, have in held[index]]
    for position in range(8):
        for index in range(count):
            block, mask = held[index][position]
            begin = ((me ^ mask) * count + index) * width
            term = contract_last(block, lax.dynamic_slice_in_dim(w_out, begin, width, 1))
            total = term if total is None else total + term
    return total


def gather_features(block):
    if lax.axis_size("tensor") != 4:
        return lax.all_gather(block, "tensor", axis=1, tiled=True)
    here = lax.axis_index("tensor")
    high, low = here // 2 == 0, here % 2 == 0
    other = swap(block, "tensor", 2)
    near = [block, other]
    far = [swap(value, "tensor", 1) for value in near]
    pairs = [
        (jnp.where(low, a, b), jnp.where(low, b, a)) for a, b in zip(near, far)
    ]
    first = [jnp.where(high, a, b) for a, b in zip(*pairs)]
    second = [jnp.where(high, b, a) for a, b in zip(*pairs)]
    return jnp.concatenate(first + second, axis=1)


def scatter_sums(total):
    if lax.axis_size("tensor") != 4:
        return lax.psum_scatter(total, "tensor", scatter_dimension=1, tiled=True)
    width = total.shape[1] // 4
    here = lax.axis_index("tensor")
    high, low = here // 2, here % 2
    kept = []
    for side in (1 - high, high):
        outgoing = lax.dynamic_slice_in_dim(total, (side * 2 + 1 - low) * width, width, 1)
        mine = lax.dynamic_slice_in_dim(total, (side * 2 + low) * width, width, 1)
        kept.append(mine + swap(outgoing.astype(jnp.bfloat16), "tensor", 1).astype(jnp.float32))
    return kept[1] + swap(kept[0].astype(jnp.bfloat16), "tensor", 2).astype(jnp.float32)


def experts_of(piece, gains, gate_w, up_w, down_w):
    values = piece.astype(jnp.float32)
    scaled = (values * gains).astype(jnp.bfloat16)
    squares_half = jnp.sum(values * values, axis=1)
    side = lax.axis_index("pipe")
    half = gate_w.shape[0] // 2
    chunks = 4 if half % 1024 == 0 else 1
    size = half // chunks

    def part(weights, whose, k):
        return lax.dynamic_slice_in_dim(weights, whose * half + k * size, size, 0)

    arrived = []
    for k in range(chunks):
        arrived.append([
            swap(contract_last(scaled, part(w, 1 - side, k)).astype(jnp.bfloat16), "pipe", 1)
            for w in (gate_w, up_w)
        ])
    squares = squares_half + swap(squares_half, "pipe", 1)
    inverse = lax.rsqrt(squares / D + EPSILON)[:, None]
    total, returned = None, []
    for k in range(chunks):
        gate, up = (
            contract_last(scaled, part(w, side, k)) + other.astype(jnp.float32)
            for w, other in zip((gate_w, up_w), arrived[k])
        )
        hidden = (jax.nn.silu(inverse * gate) * (inverse * up)).astype(jnp.bfloat16)
        returned.append(swap(hidden, "pipe", 1))
        term = jnp.dot(hidden, part(down_w, side, k), preferred_element_type=jnp.float32)
        total = term if total is None else total + term
    for k in range(chunks):
        total = total + jnp.dot(returned[k], part(down_w, 1 - side, k), preferred_element_type=jnp.float32)
    return total


def per_device(
    x_branch, z_branch, step_raw, b_matrix, c_matrix, conv_weight, conv_bias, step_bias, a_log, skip,
    w_out, residual, norm_gain, expert_ids, gate_probs, w_gate, w_up, w_down,
):
    length, channels = x_branch.shape
    feature_cols = residual.shape[1]
    experts = lax.axis_size("expert")
    slots = experts * CAP
    a_rows = a_log.T.reshape(a_log.shape[1], channels // LANES, LANES)
    rows = min(8, channels // LANES)
    gated = [
        scan_block(
            index, rows, x_branch, z_branch, step_raw, b_matrix, c_matrix, conv_weight,
            conv_bias[None, :], step_bias[None, :], a_rows, skip[None, :],
        )
        for index in range(channels // (rows * LANES))
    ]
    mamba_out = project(gated, w_out)
    stream = (residual.astype(jnp.float32) + mamba_out).astype(jnp.bfloat16)

    flat_ids = expert_ids.reshape(-1)
    member = flat_ids[:, None] == jnp.arange(experts, dtype=jnp.int32)[None, :]
    order = jnp.arange(flat_ids.shape[0], dtype=jnp.int32)
    before = jnp.dot(
        (order[:, None] > order[None, :]).astype(jnp.bfloat16),
        member.astype(jnp.bfloat16),
        preferred_element_type=jnp.float32,
    )
    position = jnp.sum(jnp.where(member, before, 0.0), axis=1).astype(jnp.int32)
    slot_ids = flat_ids * CAP + position
    matches = (
        (slot_ids[:, None] == jnp.arange(slots, dtype=jnp.int32)[None, :])
        .astype(jnp.float32)
        .reshape(length, -1, slots)
    )
    picker = jnp.sum(matches, axis=1).astype(jnp.bfloat16)
    combiner = jnp.sum(matches * gate_probs[:, :, None], axis=1)
    outgoing = contract_first(picker, stream).astype(jnp.bfloat16).reshape(experts, CAP, feature_cols)
    arrived = lax.all_to_all(outgoing, "expert", split_axis=0, concat_axis=0, tiled=True)
    piece = gather_features(arrived.reshape(slots, feature_cols))
    span = piece.shape[1]
    gains = lax.dynamic_slice_in_dim(norm_gain, lax.axis_index("pipe") * span, span, 0)
    summed = scatter_sums(experts_of(piece, gains, w_gate[0], w_up[0], w_down[0]))
    returned = lax.all_to_all(
        summed.astype(jnp.bfloat16).reshape(experts, CAP, feature_cols),
        "expert",
        split_axis=0,
        concat_axis=0,
        tiled=True,
    ).astype(jnp.float32)
    expert_mix = jnp.dot(
        combiner,
        returned.reshape(slots, feature_cols),
        precision=lax.Precision.HIGHEST,
        preferred_element_type=jnp.float32,
    )
    return (stream.astype(jnp.float32) + expert_mix).astype(jnp.bfloat16)


def solution(mesh):
    in_specs = (
        P("expert", ("pipe", "tensor")),
        P("expert", ("pipe", "tensor")),
        P("expert", ("pipe", "tensor")),
        P("expert", None),
        P("expert", None),
        P(None, ("pipe", "tensor")),
        P(("pipe", "tensor")),
        P(("pipe", "tensor")),
        P(("pipe", "tensor"), None),
        P(("pipe", "tensor")),
        P(("pipe", "tensor"), None),
        P("expert", ("pipe", "tensor")),
        P(),
        P("expert", None),
        P("expert", None),
        P("expert", "tensor", "pipe"),
        P("expert", "tensor", "pipe"),
        P("expert", "tensor", "pipe"),
    )
    out_specs = P("expert", ("pipe", "tensor"))
    return jax.shard_map(
        per_device, mesh=mesh, in_specs=in_specs, out_specs=out_specs, check_vma=False
    )
```

```python
import jax
import jax.numpy as jnp
import numpy as np
from jax import lax
from jax.experimental import pallas as pl
from jax.experimental.pallas import tpu as pltpu
from jax.sharding import PartitionSpec as P

D = 4096
CAP = 120
LANES = 128
EPSILON = 1e-05
LOG2_E = float(np.log2(np.e))


def scan_kernel(
    b_ref, c_ref, x_ref, z_ref, step_ref, taps_ref, bias_ref, step_bias_ref, a_log_ref, skip_ref,
    out_ref, padded, inner_ref, dt_ref, drive_ref, read_ref, rate_ref,
):
    length = x_ref.shape[0]
    states, rows, _ = a_log_ref.shape
    taps = taps_ref.shape[0]
    rate_ref[...] = -jnp.exp(a_log_ref[...]) * LOG2_E
    padded[0:8, :] = jnp.zeros((8, LANES), jnp.float32)
    for k in range(rows):
        cols = slice(k * LANES, (k + 1) * LANES)
        padded[8 : 8 + length, :] = x_ref[:, cols].astype(jnp.float32)
        conv = bias_ref[0:1, cols] + taps_ref[0:1, cols] * padded[9 - taps : 9 - taps + length, :]
        for offset in range(1, taps):
            begin = 9 - taps + offset
            conv = conv + taps_ref[offset : offset + 1, cols] * padded[begin : begin + length, :]
        inner = jax.nn.silu(conv)
        raw = step_ref[:, cols].astype(jnp.float32) + step_bias_ref[0:1, cols]
        dt = jnp.maximum(raw, 0.0) + jnp.log1p(jnp.exp(-jnp.abs(raw)))
        inner_ref[:, cols] = inner
        dt_ref[pl.ds(k, length, stride=rows), :] = dt
        drive_ref[pl.ds(k, length, stride=rows), :] = dt * inner

    def advance(t, state):
        here = pl.ds(pl.multiple_of(t * rows, rows), rows)
        dt, drive = dt_ref[here, :], drive_ref[here, :]
        later, sums = [], [None, None]
        for n in range(states):
            new = jnp.exp2(dt * rate_ref[n]) * state[n] + drive * b_ref[t, n]
            later.append(new)
            term = new * c_ref[t, n]
            sums[n % 2] = term if sums[n % 2] is None else sums[n % 2] + term
        read_ref[here, :] = sums[0] + sums[1]
        return tuple(later)

    lax.fori_loop(
        0, length, advance, tuple(jnp.zeros((rows, LANES), jnp.float32) for _ in range(states)), unroll=4
    )
    for k in range(rows):
        cols = slice(k * LANES, (k + 1) * LANES)
        read = read_ref[pl.ds(k, length, stride=rows), :] + skip_ref[0:1, cols] * inner_ref[:, cols]
        out_ref[:, cols] = (read * jax.nn.silu(z_ref[:, cols].astype(jnp.float32))).astype(out_ref.dtype)


def scan_block(index, rows, x, z, step, b, c, taps, bias, step_bias, a_log, skip):
    length, states = x.shape[0], a_log.shape[0]
    width = rows * LANES
    tall = pl.BlockSpec((length, width), lambda i: (0, index))
    flat = pl.BlockSpec((1, width), lambda i: (0, index))
    scalars = pl.BlockSpec(memory_space=pltpu.SMEM)
    wide = pltpu.VMEM((length * rows, LANES), jnp.float32)
    return pl.pallas_call(
        scan_kernel,
        grid=(1,),
        out_shape=jax.ShapeDtypeStruct((length, width), jnp.bfloat16),
        in_specs=[
            scalars, scalars, tall, tall, tall,
            pl.BlockSpec((taps.shape[0], width), lambda i: (0, index)), flat, flat,
            pl.BlockSpec((states, rows, LANES), lambda i: (0, index, 0)), flat,
        ],
        out_specs=pl.BlockSpec((length, width), lambda i: (0, 0)),
        scratch_shapes=[
            pltpu.VMEM((length + 8, LANES), jnp.float32),
            pltpu.VMEM((length, width), jnp.float32),
            wide, wide, wide,
            pltpu.VMEM((states, rows, LANES), jnp.float32),
        ],
        compiler_params=pltpu.CompilerParams(vmem_limit_bytes=32 * 2**20),
        cost_estimate=pl.CostEstimate(flops=10**10, bytes_accessed=2 * 10**6, transcendentals=0),
    )(b, c, x, z, step, taps, bias, step_bias, a_log, skip)


def contract_last(left, right):
    return lax.dot_general(left, right, (((1,), (1,)), ((), ())), preferred_element_type=jnp.float32)


def contract_first(left, right):
    return lax.dot_general(left, right, (((0,), (0,)), ((), ())), preferred_element_type=jnp.float32)


def swap(value, axis, mask):
    size = lax.axis_size(axis)
    return lax.ppermute(value, axis, [(i, i ^ mask) for i in range(size)])


def project(blocks, w_out):
    pipes, tensors = lax.axis_size("pipe"), lax.axis_size("tensor")
    count, width = len(blocks), blocks[0].shape[1]
    if (pipes, tensors) != (2, 4):
        whole = lax.all_gather(jnp.concatenate(blocks, axis=1), ("pipe", "tensor"), axis=1, tiled=True)
        return contract_last(whole, w_out)
    me = lax.axis_index("pipe") * tensors + lax.axis_index("tensor")
    total = None
    held = [[(block, 0)] for block in blocks]
    orders = [[("pipe", 1), ("tensor", 2), ("tensor", 1)], [("tensor", 2), ("pipe", 1), ("tensor", 1)]]
    for step in range(3):
        for index in range(count):
            axis, mask = orders[index % 2][step]
            own_mask = mask * tensors if axis == "pipe" else mask
            held[index] += [(swap(block, axis, mask), have ^ own_mask) for block, have in held[index]]
    found = [{mask: block for block, mask in blocks_held} for blocks_held in held]
    for mask in (0, 4, 2, 6, 1, 5, 3, 7):
        block = jnp.concatenate([each[mask] for each in found], axis=1)
        begin = (me ^ mask) * (count * width)
        term = contract_last(block, lax.dynamic_slice_in_dim(w_out, begin, count * width, 1))
        total = term if total is None else total + term
    return total


def gather_features(groups):
    if lax.axis_size("tensor") != 4:
        return lax.all_gather(jnp.concatenate(groups, axis=0), "tensor", axis=1, tiled=True)
    here = lax.axis_index("tensor")
    high, low = here // 2 == 0, here % 2 == 0
    found = []
    for group in groups:
        near = [group, swap(group, "tensor", 2)]
        far = [swap(value, "tensor", 1) for value in near]
        pairs = [(jnp.where(low, a, b), jnp.where(low, b, a)) for a, b in zip(near, far)]
        first = [jnp.where(high, a, b) for a, b in zip(*pairs)]
        second = [jnp.where(high, b, a) for a, b in zip(*pairs)]
        found.append(jnp.concatenate(first + second, axis=1))
    return jnp.concatenate(found, axis=0)


def scatter_sums(total):
    if lax.axis_size("tensor") != 4:
        return lax.psum_scatter(total, "tensor", scatter_dimension=1, tiled=True)
    width = total.shape[1] // 4
    here = lax.axis_index("tensor")
    high, low = here // 2, here % 2
    kept = []
    for side in (1 - high, high):
        outgoing = lax.dynamic_slice_in_dim(total, (side * 2 + 1 - low) * width, width, 1)
        mine = lax.dynamic_slice_in_dim(total, (side * 2 + low) * width, width, 1)
        kept.append(mine + swap(outgoing.astype(jnp.bfloat16), "tensor", 1).astype(jnp.float32))
    return kept[1] + swap(kept[0].astype(jnp.bfloat16), "tensor", 2).astype(jnp.float32)


def experts_of(piece, gains, gate_w, up_w, down_w):
    values = piece.astype(jnp.float32)
    scaled = (values * gains).astype(jnp.bfloat16)
    squares_half = jnp.sum(values * values, axis=1)
    side = lax.axis_index("pipe")
    half = gate_w.shape[0] // 2
    chunks = 4 if half % 1024 == 0 else 1
    size = half // chunks

    def part(weights, whose, k):
        return lax.dynamic_slice_in_dim(weights, whose * half + k * size, size, 0)

    def after(value, *earlier):
        return lax.optimization_barrier((value, *earlier))[0]

    scaled = lax.optimization_barrier(scaled)
    squares = squares_half + swap(squares_half, "pipe", 1)
    inverse = lax.rsqrt(squares / D + EPSILON)[:, None]
    arrived = []
    for k in range(chunks):
        rows = scaled if k < 2 else after(scaled, arrived[k - 2][0])
        arrived.append([
            swap(contract_last(rows, part(w, 1 - side, k)).astype(jnp.bfloat16), "pipe", 1)
            for w in (gate_w, up_w)
        ])
    owned, returned = [], []
    for k in range(chunks):
        rows = after(scaled, *arrived[max(k - 1, 0)])
        gate, up = (
            contract_last(rows, part(w, side, k)) + other.astype(jnp.float32)
            for w, other in zip((gate_w, up_w), arrived[k])
        )
        hidden = (jax.nn.silu(inverse * gate) * (inverse * up)).astype(jnp.bfloat16)
        owned.append(hidden)
        returned.append(swap(hidden, "pipe", 1))

    def down(hidden, whose, k):
        begin = whose * half + k * size
        weights = lax.dynamic_slice_in_dim(down_w, begin, hidden.shape[1], 0)
        return jnp.dot(hidden, weights, preferred_element_type=jnp.float32)

    total = down(jnp.concatenate(owned, axis=1), side, 0)
    if chunks > 1:
        total = total + down(jnp.concatenate(returned[:-1], axis=1), 1 - side, 0)
    total = lax.optimization_barrier(total)
    return total + down(returned[-1], 1 - side, chunks - 1)


def per_device(
    x_branch, z_branch, step_raw, b_matrix, c_matrix, conv_weight, conv_bias, step_bias, a_log, skip,
    w_out, residual, norm_gain, expert_ids, gate_probs, w_gate, w_up, w_down,
):
    length, channels = x_branch.shape
    feature_cols = residual.shape[1]
    experts = lax.axis_size("expert")
    slots = experts * CAP
    a_rows = a_log.T.reshape(a_log.shape[1], channels // LANES, LANES)
    rows = min(8, channels // LANES)
    gated = [
        scan_block(
            index, rows, x_branch, z_branch, step_raw, b_matrix, c_matrix, conv_weight,
            conv_bias[None, :], step_bias[None, :], a_rows, skip[None, :],
        )
        for index in range(channels // (rows * LANES))
    ]
    mamba_out = project(gated, w_out)
    stream = (residual.astype(jnp.float32) + mamba_out).astype(jnp.bfloat16)

    flat_ids = expert_ids.reshape(-1) ^ lax.axis_index("expert")
    member = flat_ids[:, None] == jnp.arange(experts, dtype=jnp.int32)[None, :]
    order = jnp.arange(flat_ids.shape[0], dtype=jnp.int32)
    before = jnp.dot(
        (order[:, None] > order[None, :]).astype(jnp.bfloat16),
        member.astype(jnp.bfloat16),
        preferred_element_type=jnp.float32,
    )
    position = jnp.sum(jnp.where(member, before, 0.0), axis=1).astype(jnp.int32)
    slot_ids = flat_ids * CAP + position
    matches = (
        (slot_ids[:, None] == jnp.arange(slots, dtype=jnp.int32)[None, :])
        .astype(jnp.float32)
        .reshape(length, -1, slots)
    )
    picker = jnp.sum(matches, axis=1).astype(jnp.bfloat16)
    combiner = jnp.sum(matches * gate_probs[:, :, None], axis=1)
    outgoing = contract_first(picker, stream).astype(jnp.bfloat16)
    near = experts // 2

    def exchange(block, number):
        return block if number == 0 else swap(block, "expert", number)

    arrived = [exchange(outgoing[number * CAP : (number + 1) * CAP], number) for number in range(experts)]
    piece = gather_features([jnp.concatenate(arrived[:near], axis=0), jnp.concatenate(arrived[near:], axis=0)])
    span = piece.shape[1]
    gains = lax.dynamic_slice_in_dim(norm_gain, lax.axis_index("pipe") * span, span, 0)
    total = experts_of(piece, gains, w_gate[0], w_up[0], w_down[0])
    returned = {}
    for begin, end in ((near, experts), (0, near)):
        summed = scatter_sums(total[begin * CAP : end * CAP]).astype(jnp.bfloat16)
        for number in range(begin, end):
            rows_back = summed[(number - begin) * CAP : (number - begin + 1) * CAP]
            returned[number] = exchange(rows_back, number)
    returned = jnp.concatenate([returned[number] for number in range(experts)], axis=0).astype(jnp.float32)
    expert_mix = jnp.dot(
        combiner,
        returned,
        precision=lax.Precision.HIGHEST,
        preferred_element_type=jnp.float32,
    )
    return (stream.astype(jnp.float32) + expert_mix).astype(jnp.bfloat16)


def solution(mesh):
    in_specs = (
        P("expert", ("pipe", "tensor")),
        P("expert", ("pipe", "tensor")),
        P("expert", ("pipe", "tensor")),
        P("expert", None),
        P("expert", None),
        P(None, ("pipe", "tensor")),
        P(("pipe", "tensor")),
        P(("pipe", "tensor")),
        P(("pipe", "tensor"), None),
        P(("pipe", "tensor")),
        P(("pipe", "tensor"), None),
        P("expert", ("pipe", "tensor")),
        P(),
        P("expert", None),
        P("expert", None),
        P("expert", "tensor", "pipe"),
        P("expert", "tensor", "pipe"),
        P("expert", "tensor", "pipe"),
    )
    out_specs = P("expert", ("pipe", "tensor"))
    return jax.shard_map(
        per_device, mesh=mesh, in_specs=in_specs, out_specs=out_specs, check_vma=False
    )
```

```python
import jax
import jax.numpy as jnp
import numpy as np
from jax import lax
from jax.experimental import pallas as pl
from jax.experimental.pallas import tpu as pltpu
from jax.sharding import PartitionSpec as P

D = 4096
CAP = 120
LANES = 128
EPSILON = 1e-05
LOG2_E = float(np.log2(np.e))


def scan_kernel(
    b_ref, c_ref, x_ref, z_ref, step_ref, taps_ref, bias_ref, step_bias_ref, a_log_ref, skip_ref,
    out_ref, padded, inner_ref, dt_ref, drive_ref, read_ref, rate_ref,
):
    length = x_ref.shape[0]
    states, rows, _ = a_log_ref.shape
    taps = taps_ref.shape[0]
    rate_ref[...] = -jnp.exp(a_log_ref[...]) * LOG2_E
    padded[0:8, :] = jnp.zeros((8, LANES), jnp.float32)
    for k in range(rows):
        cols = slice(k * LANES, (k + 1) * LANES)
        padded[8 : 8 + length, :] = x_ref[:, cols].astype(jnp.float32)
        conv = bias_ref[0:1, cols] + taps_ref[0:1, cols] * padded[9 - taps : 9 - taps + length, :]
        for offset in range(1, taps):
            begin = 9 - taps + offset
            conv = conv + taps_ref[offset : offset + 1, cols] * padded[begin : begin + length, :]
        inner = jax.nn.silu(conv)
        raw = step_ref[:, cols].astype(jnp.float32) + step_bias_ref[0:1, cols]
        dt = jnp.maximum(raw, 0.0) + jnp.log1p(jnp.exp(-jnp.abs(raw)))
        inner_ref[:, cols] = inner
        dt_ref[pl.ds(k, length, stride=rows), :] = dt
        drive_ref[pl.ds(k, length, stride=rows), :] = dt * inner

    def advance(t, state):
        here = pl.ds(pl.multiple_of(t * rows, rows), rows)
        dt, drive = dt_ref[here, :], drive_ref[here, :]
        later, sums = [], [None, None]
        for n in range(states):
            new = jnp.exp2(dt * rate_ref[n]) * state[n] + drive * b_ref[t, n]
            later.append(new)
            term = new * c_ref[t, n]
            sums[n % 2] = term if sums[n % 2] is None else sums[n % 2] + term
        read_ref[here, :] = sums[0] + sums[1]
        return tuple(later)

    lax.fori_loop(
        0, length, advance, tuple(jnp.zeros((rows, LANES), jnp.float32) for _ in range(states)), unroll=4
    )
    for k in range(rows):
        cols = slice(k * LANES, (k + 1) * LANES)
        read = read_ref[pl.ds(k, length, stride=rows), :] + skip_ref[0:1, cols] * inner_ref[:, cols]
        out_ref[:, cols] = (read * jax.nn.silu(z_ref[:, cols].astype(jnp.float32))).astype(out_ref.dtype)


def scan_block(index, rows, x, z, step, b, c, taps, bias, step_bias, a_log, skip):
    length, states = x.shape[0], a_log.shape[0]
    width = rows * LANES
    tall = pl.BlockSpec((length, width), lambda i: (0, index))
    flat = pl.BlockSpec((1, width), lambda i: (0, index))
    scalars = pl.BlockSpec(memory_space=pltpu.SMEM)
    wide = pltpu.VMEM((length * rows, LANES), jnp.float32)
    return pl.pallas_call(
        scan_kernel,
        grid=(1,),
        out_shape=jax.ShapeDtypeStruct((length, width), jnp.bfloat16),
        in_specs=[
            scalars, scalars, tall, tall, tall,
            pl.BlockSpec((taps.shape[0], width), lambda i: (0, index)), flat, flat,
            pl.BlockSpec((states, rows, LANES), lambda i: (0, index, 0)), flat,
        ],
        out_specs=pl.BlockSpec((length, width), lambda i: (0, 0)),
        scratch_shapes=[
            pltpu.VMEM((length + 8, LANES), jnp.float32),
            pltpu.VMEM((length, width), jnp.float32),
            wide, wide, wide,
            pltpu.VMEM((states, rows, LANES), jnp.float32),
        ],
        compiler_params=pltpu.CompilerParams(vmem_limit_bytes=32 * 2**20),
        cost_estimate=pl.CostEstimate(flops=10**10, bytes_accessed=2 * 10**6, transcendentals=0),
    )(b, c, x, z, step, taps, bias, step_bias, a_log, skip)


def contract_last(left, right):
    return lax.dot_general(left, right, (((1,), (1,)), ((), ())), preferred_element_type=jnp.float32)


def contract_first(left, right):
    return lax.dot_general(left, right, (((0,), (0,)), ((), ())), preferred_element_type=jnp.float32)


def swap(value, axis, mask):
    size = lax.axis_size(axis)
    return lax.ppermute(value, axis, [(i, i ^ mask) for i in range(size)])


def project(blocks, w_out):
    pipes, tensors = lax.axis_size("pipe"), lax.axis_size("tensor")
    count, width = len(blocks), blocks[0].shape[1]
    if (pipes, tensors) != (2, 4):
        whole = lax.all_gather(jnp.concatenate(blocks, axis=1), ("pipe", "tensor"), axis=1, tiled=True)
        return contract_last(whole, w_out)
    me = lax.axis_index("pipe") * tensors + lax.axis_index("tensor")
    total = None
    held = [[(block, 0)] for block in blocks]
    orders = [[("pipe", 1), ("tensor", 2), ("tensor", 1)], [("tensor", 2), ("pipe", 1), ("tensor", 1)]]
    for step in range(3):
        for index in range(count):
            axis, mask = orders[index % 2][step]
            own_mask = mask * tensors if axis == "pipe" else mask
            held[index] += [(swap(block, axis, mask), have ^ own_mask) for block, have in held[index]]
    found = [{mask: block for block, mask in blocks_held} for blocks_held in held]
    for mask in (0, 4, 2, 6, 1, 5, 3, 7):
        block = jnp.concatenate([each[mask] for each in found], axis=1)
        begin = (me ^ mask) * (count * width)
        term = contract_last(block, lax.dynamic_slice_in_dim(w_out, begin, count * width, 1))
        total = term if total is None else total + term
    return total


def gather_features(groups):
    if lax.axis_size("tensor") != 4:
        return lax.all_gather(jnp.concatenate(groups, axis=0), "tensor", axis=1, tiled=True)
    here = lax.axis_index("tensor")
    high, low = here // 2 == 0, here % 2 == 0
    near = [[group, swap(group, "tensor", 2)] for group in groups]
    far = [[swap(value, "tensor", 1) for value in pair] for pair in near]
    near, far = ([jnp.concatenate(rows, axis=0) for rows in zip(*pairs)] for pairs in (near, far))
    near, far = lax.optimization_barrier((near, far))
    pairs = [(jnp.where(low, a, b), jnp.where(low, b, a)) for a, b in zip(near, far)]
    first = [jnp.where(high, a, b) for a, b in zip(*pairs)]
    second = [jnp.where(high, b, a) for a, b in zip(*pairs)]
    return jnp.concatenate(first + second, axis=1)


def scatter_sums(total):
    if lax.axis_size("tensor") != 4:
        return lax.psum_scatter(total, "tensor", scatter_dimension=1, tiled=True)
    width = total.shape[1] // 4
    here = lax.axis_index("tensor")
    high, low = here // 2, here % 2
    kept = []
    for side in (1 - high, high):
        outgoing = lax.dynamic_slice_in_dim(total, (side * 2 + 1 - low) * width, width, 1)
        mine = lax.dynamic_slice_in_dim(total, (side * 2 + low) * width, width, 1)
        kept.append(mine + swap(outgoing.astype(jnp.bfloat16), "tensor", 1).astype(jnp.float32))
    return kept[1] + swap(kept[0].astype(jnp.bfloat16), "tensor", 2).astype(jnp.float32)


def experts_of(piece, gains, gate_w, up_w, down_w):
    values = piece.astype(jnp.float32)
    scaled = (values * gains).astype(jnp.bfloat16)
    squares_half = jnp.sum(values * values, axis=1)
    side = lax.axis_index("pipe")
    half = gate_w.shape[0] // 2
    chunks = 4 if half % 1024 == 0 else 1
    size = half // chunks

    def part(weights, whose, k):
        return lax.dynamic_slice_in_dim(weights, whose * half + k * size, size, 0)

    def after(value, *earlier):
        return lax.optimization_barrier((value, *earlier))[0]

    scaled = lax.optimization_barrier(scaled)
    squares = squares_half + swap(squares_half, "pipe", 1)
    inverse = lax.rsqrt(squares / D + EPSILON)[:, None]
    arrived = []
    for k in range(chunks):
        rows = scaled if k < 2 else after(scaled, arrived[k - 2][0])
        arrived.append([
            swap(contract_last(rows, part(w, 1 - side, k)).astype(jnp.bfloat16), "pipe", 1)
            for w in (gate_w, up_w)
        ])
    owned, returned = [], []
    for k in range(chunks):
        rows = after(scaled, *arrived[max(k - 1, 0)])
        gate, up = (
            contract_last(rows, part(w, side, k)) + other.astype(jnp.float32)
            for w, other in zip((gate_w, up_w), arrived[k])
        )
        hidden = (jax.nn.silu(inverse * gate) * (inverse * up)).astype(jnp.bfloat16)
        owned.append(hidden)
        returned.append(swap(hidden, "pipe", 1))

    def down(hidden, whose, k):
        begin = whose * half + k * size
        weights = lax.dynamic_slice_in_dim(down_w, begin, hidden.shape[1], 0)
        return jnp.dot(hidden, weights, preferred_element_type=jnp.float32)

    total = down(jnp.concatenate(owned, axis=1), side, 0)
    if chunks > 1:
        total = total + down(jnp.concatenate(returned[:-1], axis=1), 1 - side, 0)
    total = lax.optimization_barrier(total)
    return total + down(returned[-1], 1 - side, chunks - 1)


def per_device(
    x_branch, z_branch, step_raw, b_matrix, c_matrix, conv_weight, conv_bias, step_bias, a_log, skip,
    w_out, residual, norm_gain, expert_ids, gate_probs, w_gate, w_up, w_down,
):
    length, channels = x_branch.shape
    feature_cols = residual.shape[1]
    experts = lax.axis_size("expert")
    slots = experts * CAP
    a_rows = a_log.T.reshape(a_log.shape[1], channels // LANES, LANES)
    rows = min(8, channels // LANES)
    gated = [
        scan_block(
            index, rows, x_branch, z_branch, step_raw, b_matrix, c_matrix, conv_weight,
            conv_bias[None, :], step_bias[None, :], a_rows, skip[None, :],
        )
        for index in range(channels // (rows * LANES))
    ]
    mamba_out = project(gated, w_out)
    stream = (residual.astype(jnp.float32) + mamba_out).astype(jnp.bfloat16)

    flat_ids = expert_ids.reshape(-1) ^ lax.axis_index("expert")
    member = flat_ids[:, None] == jnp.arange(experts, dtype=jnp.int32)[None, :]
    order = jnp.arange(flat_ids.shape[0], dtype=jnp.int32)
    before = jnp.dot(
        (order[:, None] > order[None, :]).astype(jnp.bfloat16),
        member.astype(jnp.bfloat16),
        preferred_element_type=jnp.float32,
    )
    position = jnp.sum(jnp.where(member, before, 0.0), axis=1).astype(jnp.int32)
    slot_ids = flat_ids * CAP + position
    matches = (
        (slot_ids[:, None] == jnp.arange(slots, dtype=jnp.int32)[None, :])
        .astype(jnp.float32)
        .reshape(length, -1, slots)
    )
    picker = jnp.sum(matches, axis=1).astype(jnp.bfloat16)
    combiner = jnp.sum(matches * gate_probs[:, :, None], axis=1)
    outgoing = contract_first(picker, stream).astype(jnp.bfloat16)
    near = experts // 2

    def exchange(block, number):
        return block if number == 0 else swap(block, "expert", number)

    arrived = [exchange(outgoing[number * CAP : (number + 1) * CAP], number) for number in range(experts)]
    piece = gather_features([jnp.concatenate(arrived[:near], axis=0), jnp.concatenate(arrived[near:], axis=0)])
    span = piece.shape[1]
    gains = lax.dynamic_slice_in_dim(norm_gain, lax.axis_index("pipe") * span, span, 0)
    total = experts_of(piece, gains, w_gate[0], w_up[0], w_down[0])
    returned = {}
    for begin, end in ((near, experts), (0, near)):
        summed = scatter_sums(total[begin * CAP : end * CAP]).astype(jnp.bfloat16)
        for number in range(begin, end):
            rows_back = summed[(number - begin) * CAP : (number - begin + 1) * CAP]
            returned[number] = exchange(rows_back, number)
    returned = jnp.concatenate([returned[number] for number in range(experts)], axis=0).astype(jnp.float32)
    expert_mix = jnp.dot(
        combiner,
        returned,
        precision=lax.Precision.HIGHEST,
        preferred_element_type=jnp.float32,
    )
    return (stream.astype(jnp.float32) + expert_mix).astype(jnp.bfloat16)


def solution(mesh):
    in_specs = (
        P("expert", ("pipe", "tensor")),
        P("expert", ("pipe", "tensor")),
        P("expert", ("pipe", "tensor")),
        P("expert", None),
        P("expert", None),
        P(None, ("pipe", "tensor")),
        P(("pipe", "tensor")),
        P(("pipe", "tensor")),
        P(("pipe", "tensor"), None),
        P(("pipe", "tensor")),
        P(("pipe", "tensor"), None),
        P("expert", ("pipe", "tensor")),
        P(),
        P("expert", None),
        P("expert", None),
        P("expert", "tensor", "pipe"),
        P("expert", "tensor", "pipe"),
        P("expert", "tensor", "pipe"),
    )
    out_specs = P("expert", ("pipe", "tensor"))
    return jax.shard_map(
        per_device, mesh=mesh, in_specs=in_specs, out_specs=out_specs, check_vma=False
    )
```
